32 devices in a mesh: video: 2 (over y), rows: 4 (over z), cols: 4 (over x, core).
Axes of the slice: x: 2, y: 2, z: 4, core: 2. Of those that a mesh axis runs over, the one named last changes fastest.
Arguments:
- frame_in: bfloat16 [64, 80, 512], P(('video', 'rows'), 'cols'), parts along dimension 0, may hold values from -6 to 6
- norm_gain: float32 [512], replicated, may hold values from 0.5 to 1.5
- w_query: bfloat16 [512, 512], replicated, may hold values from -2 to 2
- w_key: bfloat16 [512, 512], replicated, may hold values from -0.125 to 0.125
- w_value: bfloat16 [512, 512], replicated, may hold values from -0.25 to 0.25
- w_out: bfloat16 [512, 512], replicated, may hold values from -0.25 to 0.25
- conv_gain: float32 [512], replicated, may hold values from 0.5 to 1.5
- conv_cache: bfloat16 [2, 64, 80, 512], P(None, ('video', 'rows'), 'cols'), parts along dimension 1, may hold values from -6 to 6
- w_conv: bfloat16 [3, 3, 3, 512, 256], replicated, may hold values from -0.0546875 to 0.0546875
- conv_bias: float32 [256], replicated, may hold values from -0.5 to 0.5
Outputs:
- hidden: bfloat16 [64, 80, 512], P(('video', 'rows'), 'cols'), parts along dimension 0
- mixed_out: bfloat16 [64, 80, 256], P(('video', 'rows'), 'cols'), parts along dimension 0
The draws below stay inside these ranges and needn't reach their ends.
There are 2 independent parts, one for each index of `video`. The reference program is written for one: setup_inputs(seed, part) draws one part's arguments, and reference() takes and returns one part's arrays. A program takes and returns all parts, laid end to end along the dimension named above; an argument that names none is the same for every part. Nothing has to cross between parts.
All inputs are finite; a program needn't handle non-finite values.
Results may differ from the reference program's by a relative error of at most 0.012.
Values may be sent and summed in bfloat16 or wider, within the bound.
A program may use at most 128 MiB of HBM per device.

```python
import math
import jax
import jax.numpy as jnp
from jax import lax

C = 512
CO = 256
H = 32
W = 80


def weight_bases(key):
    inner = jax.random.fold_in(key, 4711)
    first_key, second_key = jax.random.split(inner)
    shared = jax.random.normal(first_key, (C, C), jnp.float32)
    others = jax.random.normal(second_key, (C, C), jnp.float32)
    return (shared, others)


def draw_w_key(key, part):
    shared, others = weight_bases(key)
    return jnp.clip(shared * (1.0 / math.sqrt(C)), -0.125, 0.125).astype(jnp.bfloat16)


def draw_w_query(key, part):
    shared, others = weight_bases(key)
    mixed_vals = jnp.clip(others * (1.0 / math.sqrt(C)), -0.125, 0.125)
    return mixed_vals.astype(jnp.bfloat16)


def draw_frame_in(key, part):
    base_key = jax.random.fold_in(key, 0)
    base = jnp.clip(jax.random.normal(base_key, (H, W, C), jnp.float32), -6.0, 6.0)
    return base.astype(jnp.bfloat16)


def level_of(rng, extent, shards, low, top_value):
    def one(dim, parts):
        heights = jax.random.uniform(jax.random.fold_in(jax.random.fold_in(rng, 6), dim), (parts,), jnp.float32, low / len(shards), top_value / len(shards))
        return jnp.repeat(jnp.exp(heights), extent[dim] // parts).reshape((-1,) + (1,) * (len(extent) - dim - 1))

    level = one(*shards[0])
    for cut in shards[1:]:
        level = level * one(*cut)
    return level


def bell_draw(own_key, dims, spread, most, shards=(), dtype=jnp.bfloat16):
    result = spread * jax.random.normal(own_key, dims, jnp.float32)
    if shards:
        result = result * level_of(own_key, dims, shards, -0.22, 0.18)
    return jnp.clip(result, -most, most).astype(dtype)


def setup_inputs(seed: int = 0, part: int = 0) -> dict:
    key_list = jax.random.split(jax.random.key(seed), 11)
    part_keys = jax.random.split(jax.random.fold_in(key_list[10], part), 11)
    return {
        "frame_in": draw_frame_in(jax.random.fold_in(jax.random.fold_in(key_list[10], part), 71), part),
        "norm_gain": jnp.clip(jax.random.uniform(key_list[1], (C,), jnp.float32, 0.5, 1.5), 0.5, 1.5),
        "w_query": draw_w_query(jax.random.fold_in(key_list[10], 71), part),
        "w_key": draw_w_key(jax.random.fold_in(key_list[10], 71), part),
        "w_value": bell_draw(key_list[4], (C, C), C ** -0.5, 0.25),
        "w_out": bell_draw(key_list[5], (C, C), C ** -0.5, 0.25),
        "conv_gain": jnp.clip(jax.random.uniform(key_list[6], (C,), jnp.float32, 0.5, 1.5), 0.5, 1.5),
        "conv_cache": bell_draw(part_keys[7], (2, H, W, C), 1.0, 6.0, ((1, 4), (2, 4))),
        "w_conv": bell_draw(key_list[8], (3, 3, 3, C, CO), (27 * C) ** -0.5, 0.0546875),
        "conv_bias": jnp.clip(jax.random.uniform(key_list[9], (CO,), jnp.float32, -0.5, 0.5), -0.5, 0.5),
    }


def rms_scaled(values, gain):
    mean_sq = lax.optimization_barrier(jnp.mean(values * values, axis=-1, keepdims=True))
    return values * lax.rsqrt(mean_sq + 1e-06) * gain

def reference(frame_in, norm_gain, w_query, w_key, w_value, w_out, conv_gain, conv_cache, w_conv, conv_bias):
    tokens = frame_in.astype(jnp.float32).reshape(H * W, C)
    normed = rms_scaled(tokens, norm_gain).astype(jnp.bfloat16)
    query_rows = (jnp.dot(normed, w_query, preferred_element_type=jnp.float32) * (1.0 / math.sqrt(C))).astype(jnp.bfloat16)
    query_keys = jnp.dot(query_rows, w_key.T, preferred_element_type=jnp.float32).astype(jnp.bfloat16)

    def one_row(query_block):
        scores = jnp.dot(query_block, normed.T, preferred_element_type=jnp.float32)
        peak = lax.optimization_barrier(jnp.max(scores, axis=1, keepdims=True))
        weights = jnp.exp(scores - peak)
        total_sum = lax.optimization_barrier(jnp.sum(weights, axis=1, keepdims=True))
        summed = jnp.dot(weights.astype(jnp.bfloat16), normed, preferred_element_type=jnp.float32)
        return (summed / total_sum).astype(jnp.bfloat16)
    pooled = lax.map(one_row, query_keys.reshape(H, W, C)).reshape(H * W, C)
    attended = jnp.dot(pooled, w_value, preferred_element_type=jnp.float32).astype(jnp.bfloat16)
    hidden = (tokens + jnp.dot(attended, w_out, preferred_element_type=jnp.float32)).astype(jnp.bfloat16)
    conv_input = jax.nn.silu(rms_scaled(hidden.astype(jnp.float32), conv_gain)).astype(jnp.bfloat16)
    stacked = jnp.concatenate([conv_cache, conv_input.reshape(1, H, W, C)], axis=0)
    padded = jnp.pad(stacked, ((0, 0), (1, 1), (1, 1), (0, 0)))
    result_sum = hidden[:, :CO].astype(jnp.float32) + conv_bias
    for time_off in range(3):
        for row_off in range(3):
            for col_off in range(3):
                window = padded[time_off, row_off:row_off + H, col_off:col_off + W, :].reshape(H * W, C)
                result_sum = result_sum + jnp.dot(window, w_conv[time_off, row_off, col_off], preferred_element_type=jnp.float32)
    return (hidden.reshape(H, W, C), result_sum.astype(jnp.bfloat16).reshape(H, W, CO))
```

```python
import functools
import math

import jax
import jax.numpy as jnp
from jax import lax
from jax.experimental import pallas as pl
from jax.experimental.pallas import tpu as pltpu
from jax.sharding import PartitionSpec as P

MESH = pl.DeviceIdType.MESH
F32 = jnp.float32
BF16 = jnp.bfloat16
PITCH = 32


def rms_scaled(values, gain):
    mean_sq = jnp.mean(values * values, axis=-1, keepdims=True)
    return values * lax.rsqrt(mean_sq + 1e-06) * gain


def kernel(
    rows, cols, frame_ref, ngain_ref, wq_hbm, wk_hbm, wv_hbm, wo_hbm, cgain_ref, cache_hbm, wc_hbm, bias_ref,
    hidden_ref, mixed_ref,
    wq, wk, wv, wo, wc, cache, kv, tok, qk, acc, peak, total, xp, col_out, col_in, sums,
    load_sem, z_send, x_send, d_send, recv_sem, halo_send, halo_recv,
):
    tile_rows, tile_cols, channels = frame_ref.shape
    out_channels = wc.shape[-1]
    count = tile_rows * tile_cols
    v, r, c = lax.axis_index("video"), lax.axis_index("rows"), lax.axis_index("cols")
    nx = cols // 2
    x, lane = c // 2, c % 2
    sibling = x * 2 + 1 - lane
    me = r * cols + c

    loads = [
        pltpu.make_async_copy(src, dst, load_sem.at[n])
        for n, (src, dst) in enumerate(
            [(cache_hbm, cache), (wq_hbm, wq), (wk_hbm, wk), (wc_hbm, wc), (wv_hbm, wv), (wo_hbm, wo)]
        )
    ]
    for load in loads:
        load.start()

    barrier = pltpu.get_barrier_semaphore()

    @pl.loop(0, rows * cols)
    def _(d):
        @pl.when(d != me)
        def _():
            pl.semaphore_signal(barrier, inc=1, device_id=(v, d // cols, d % cols), device_id_type=MESH)

    for q in range(tile_rows):
        tok[pl.ds(q * tile_cols, tile_cols), :] = frame_ref[q].astype(F32)
    normed = rms_scaled(tok[...], ngain_ref[...]).astype(BF16)
    kv[me] = normed

    pl.semaphore_wait(barrier, rows * cols - 1)

    def push(slot, row, col, send_sem):
        return pltpu.make_async_remote_copy(
            src_ref=kv.at[slot], dst_ref=kv.at[slot], send_sem=send_sem, recv_sem=recv_sem.at[slot],
            device_id=(v, row, col), device_id_type=MESH,
        )

    def z_copy(k):
        return push(me, (r + rows - k) % rows, c, z_send.at[k])

    def x_copy(k, d):
        slot = ((r + k) % rows) * cols + c
        return push(slot, r, ((x + d) % nx) * 2 + lane, x_send.at[k, d])

    def d_copy(k, d):
        slot = ((r + k) % rows) * cols + ((x + d) % nx) * 2 + lane
        return push(slot, r, sibling, d_send.at[k, d])

    def arrived(slot):
        push(slot, r, sibling, d_send.at[0, 0]).wait_recv()

    def spread(k):
        for d in range(1, nx):
            x_copy(k, d).start()
        d_copy(k, 0).start()

    for k in range(1, rows):
        z_copy(k).start()
    spread(0)

    def halo_copies(phase, first, times):
        span = pl.ds(first, times)
        jobs = []
        for n, (src, dst, dr) in enumerate([(tile_rows, 0, 1), (1, tile_rows + 1, -1)]):
            jobs.append((xp.at[span, src], xp.at[span, dst], dr, 0, n))
        for side, dc in ((0, 1), (1, -1)):
            for dr in (-1, 0, 1):
                jobs.append((col_out.at[span, side], col_in.at[span, side, 1 - dr], dr, dc, 2 + side * 3 + dr + 1))
        made = []
        for src, dst, dr, dc, n in jobs:
            to_row, to_col, from_row, from_col = r + dr, c + dc, r - dr, c - dc
            sends = (to_row >= 0) & (to_row < rows) & (to_col >= 0) & (to_col < cols)
            gets = (from_row >= 0) & (from_row < rows) & (from_col >= 0) & (from_col < cols)
            copy = pltpu.make_async_remote_copy(
                src_ref=src, dst_ref=dst, send_sem=halo_send.at[phase, n], recv_sem=halo_recv.at[phase, n],
                device_id=(v, lax.select(sends, to_row, r), lax.select(sends, to_col, c)), device_id_type=MESH,
            )
            made.append((copy, dst, sends, gets))
        return made

    def place(t, load_row):
        pad_low = jnp.zeros((1, channels), F32)
        pad_high = jnp.zeros((PITCH - tile_cols - 1, channels), F32)
        for q in range(tile_rows):
            xp[t, q + 1] = jnp.concatenate([pad_low, load_row(q), pad_high], axis=0).astype(BF16)

    def set_columns(t, ends):
        blank = jnp.zeros((tile_rows, channels), F32)
        for side, column in enumerate(ends):
            col_out[t, side] = jnp.concatenate([column, blank], axis=0).astype(BF16)

    def send_halo(copies):
        for copy, dst, sends, gets in copies:
            pl.when(sends)(copy.start)

            @pl.when(jnp.logical_not(gets))
            def _(dst=dst):
                dst[...] = jnp.zeros(dst.shape, BF16)

    def take_halo(copies):
        for copy, dst, sends, gets in copies:
            pl.when(gets)(copy.wait_recv)
            pl.when(sends)(copy.wait_send)

    def insert_columns(t):
        at = lax.broadcasted_iota(jnp.int32, (PITCH, channels), 0)
        ends = []
        for side in range(2):
            above, beside, below = (col_in[t, side, n].astype(F32) for n in range(3))
            ends.append(
                [above[tile_rows - 1 : tile_rows]] + [beside[q : q + 1] for q in range(tile_rows)] + [below[:1]]
            )
        for q in range(tile_rows + 2):
            row = xp[t, q].astype(F32)
            row = jnp.where(at == 0, ends[0][q], jnp.where(at == tile_cols + 1, ends[1][q], row))
            xp[t, q] = row.astype(BF16)

    def convolve(t, fresh):
        lines = [xp[t, i : i + tile_rows].reshape(tile_rows * PITCH, channels) for i in range(3)]
        for j in range(3):
            part = sum(jnp.dot(lines[i], wc[t, i, j], preferred_element_type=F32) for i in range(3))
            if fresh:
                sums[j] = part
            else:
                sums[j] += part

    loads[0].wait()
    for t in range(2):
        place(t, lambda q: cache[t, q].astype(F32))
        tile = [cache[t, q].astype(F32) for q in range(tile_rows)]
        set_columns(
            t,
            [
                jnp.concatenate([line[tile_cols - 1 :] for line in tile], axis=0),
                jnp.concatenate([line[:1] for line in tile], axis=0),
            ],
        )
    cache_halo = halo_copies(0, 0, 2)
    send_halo(cache_halo)

    loads[1].wait()
    loads[2].wait()
    query = (jnp.dot(normed, wq[...], preferred_element_type=F32) * (1.0 / math.sqrt(channels))).astype(BF16)
    qk[...] = lax.dot_general(query, wk[...], (((1,), (1,)), ((), ())), preferred_element_type=F32).astype(BF16)
    peak[...] = jnp.full(peak.shape, -1e30, F32)
    total[...] = jnp.zeros(total.shape, F32)
    acc[...] = jnp.zeros(acc.shape, F32)

    take_halo(cache_halo)
    loads[3].wait()
    for t in range(2):
        insert_columns(t)
        convolve(t, t == 0)

    def cross(k):
        for d in range(1, nx):
            arrived(((r + k) % rows) * cols + ((x + d) % nx) * 2 + lane)
            d_copy(k, d).start()

    def attend(k):
        row = (r + k) % rows
        for d in range(nx):
            arrived(row * cols + d * 2 + 1 - lane)
        keys = kv[pl.ds(row * cols, cols)].reshape(cols * count, channels)
        scores = lax.dot_general(qk[...], keys, (((1,), (1,)), ((), ())), preferred_element_type=F32)
        old = peak[:, :1]
        new = jnp.maximum(old, jnp.max(scores, axis=1, keepdims=True))
        weights = jnp.exp(scores - new)
        scale = jnp.exp(old - new)
        total[...] = jnp.broadcast_to(total[:, :1] * scale + jnp.sum(weights, axis=1, keepdims=True), total.shape)
        acc[...] = acc[...] * scale + jnp.dot(weights.astype(BF16), keys, preferred_element_type=F32)
        peak[...] = jnp.broadcast_to(new, peak.shape)

    @pl.loop(1, rows)
    def _(k):
        arrived(((r + k) % rows) * cols + c)
        spread(k)
        cross(k - 1)
        attend(k - 1)

    cross(rows - 1)
    attend(rows - 1)

    loads[4].wait()
    loads[5].wait()
    pooled = (acc[...] / total[:, :1]).astype(BF16)
    attended = jnp.dot(pooled, wv[...], preferred_element_type=F32).astype(BF16)
    hidden = (tok[...] + jnp.dot(attended, wo[...], preferred_element_type=F32)).astype(BF16)
    hidden32 = hidden.astype(F32)
    tok[...] = hidden32
    scaled = rms_scaled(hidden32, cgain_ref[...])
    acc[...] = scaled / (1.0 + jnp.exp(-scaled))
    place(2, lambda q: acc[pl.ds(q * tile_cols, tile_cols), :])
    set_columns(
        2, [
            jnp.concatenate([acc[pl.ds(q * tile_cols + e, 1), :] for q in range(tile_rows)], axis=0)
            for e in (tile_cols - 1, 0)
        ]
    )
    frame_halo = halo_copies(1, 2, 1)
    send_halo(frame_halo)
    for q in range(tile_rows):
        hidden_ref[q] = tok[pl.ds(q * tile_cols, tile_cols), :].astype(BF16)
    take_halo(frame_halo)
    insert_columns(2)
    convolve(2, False)
    for q in range(tile_rows):
        line = tok[pl.ds(q * tile_cols, tile_cols), :out_channels] + bias_ref[...]
        for j in range(3):
            line = line + sums[j, pl.ds(q * PITCH + j, tile_cols), :]
        mixed_ref[q] = line.astype(BF16)

    for k in range(1, rows):
        z_copy(k).wait_send()

    @pl.loop(0, rows)
    def _(k):
        for d in range(1, nx):
            x_copy(k, d).wait_send()
        for d in range(nx):
            d_copy(k, d).wait_send()


def solution(mesh):
    rows, cols = mesh.shape["rows"], mesh.shape["cols"]

    def body(frame_in, norm_gain, w_query, w_key, w_value, w_out, conv_gain, conv_cache, w_conv, conv_bias):
        tile_rows, tile_cols, channels = frame_in.shape
        out_channels = w_conv.shape[-1]
        count = tile_rows * tile_cols
        wide = tile_rows * PITCH
        vmem, held = pl.BlockSpec(memory_space=pltpu.VMEM), pl.BlockSpec(memory_space=pl.ANY)
        dma = pltpu.SemaphoreType.DMA
        square = pltpu.VMEM((channels, channels), BF16)
        return pl.pallas_call(
            functools.partial(kernel, rows, cols),
            out_shape=(
                jax.ShapeDtypeStruct(frame_in.shape, BF16),
                jax.ShapeDtypeStruct((tile_rows, tile_cols, out_channels), BF16),
            ),
            in_specs=[vmem, vmem, held, held, held, held, vmem, held, held, vmem],
            out_specs=(vmem, vmem),
            scratch_shapes=[
                square, square, square, square,
                pltpu.VMEM(w_conv.shape, BF16),
                pltpu.VMEM(conv_cache.shape, BF16),
                pltpu.VMEM((rows * cols, count, channels), BF16),
                pltpu.VMEM((count, channels), F32),
                pltpu.VMEM((count, channels), BF16),
                pltpu.VMEM((count, channels), F32),
                pltpu.VMEM((count, 128), F32),
                pltpu.VMEM((count, 128), F32),
                pltpu.VMEM((3, tile_rows + 2, PITCH, channels), BF16),
                pltpu.VMEM((3, 2, 2 * tile_rows, channels), BF16),
                pltpu.VMEM((3, 2, 3, 2 * tile_rows, channels), BF16),
                pltpu.VMEM((3, wide, out_channels), F32),
                dma((6,)), dma((rows,)), dma((rows, cols // 2)), dma((rows, cols // 2)), dma((rows * cols,)),
                dma((2, 8)), dma((2, 8)),
            ],
            compiler_params=pltpu.CompilerParams(
                collective_id=0, has_side_effects=True, vmem_limit_bytes=56 * 1024 * 1024
            ),
        )(
            frame_in, norm_gain.reshape(1, channels), w_query, w_key, w_value, w_out,
            conv_gain.reshape(1, channels), conv_cache, w_conv, conv_bias.reshape(1, out_channels),
        )

    tiles = P(("video", "rows"), "cols", None)
    in_specs = (tiles, P(), P(), P(), P(), P(), P(), P(None, ("video", "rows"), "cols", None), P(), P())
    return jax.shard_map(body, mesh=mesh, in_specs=in_specs, out_specs=(tiles, tiles), check_vma=False)
```

```python
import functools
import math

import jax
import jax.numpy as jnp
from jax import lax
from jax.experimental import pallas as pl
from jax.experimental.pallas import tpu as pltpu
from jax.sharding import PartitionSpec as P

MESH = pl.DeviceIdType.MESH
F32 = jnp.float32
BF16 = jnp.bfloat16


def rms_scaled(values, gain):
    mean_sq = jnp.mean(values * values, axis=-1, keepdims=True)
    return values * lax.rsqrt(mean_sq + 1e-06) * gain


def kernel(
    rows, cols, frame_ref, ngain_ref, wq_hbm, wk_hbm, wv_hbm, wo_hbm, cgain_ref, cache_hbm, wc_hbm, bias_ref,
    hidden_ref, mixed_ref,
    wq, wk, wv, wo, wc, cache, kv, tok, qk, acc, peak, total, pad, flat, row_out, row_in, col_in, even, odd, sums,
    load_sem, z_send, x_send, d_send, recv_sem, halo_send, halo_recv,
):
    tile_cols, tile_rows, channels = frame_ref.shape
    out_channels = wc.shape[-1]
    count = tile_rows * tile_cols
    v, r, c = lax.axis_index("video"), lax.axis_index("rows"), lax.axis_index("cols")
    nx = cols // 2
    x, lane = c // 2, c % 2
    sibling = x * 2 + 1 - lane
    me = r * cols + c
    parts = [(n, slice(n * 128, n * 128 + 128)) for n in range(channels // 128)]

    loads = [
        pltpu.make_async_copy(src, dst, load_sem.at[n])
        for n, (src, dst) in enumerate(
            [(cache_hbm, cache), (wq_hbm, wq), (wk_hbm, wk), (wc_hbm, wc), (wv_hbm, wv), (wo_hbm, wo)]
        )
    ]
    for load in loads:
        load.start()

    barrier = pltpu.get_barrier_semaphore()

    @pl.loop(0, rows * cols)
    def _(d):
        @pl.when(d != me)
        def _():
            pl.semaphore_signal(barrier, inc=1, device_id=(v, d // cols, d % cols), device_id_type=MESH)

    tok[...] = frame_ref[...].astype(F32).reshape(count, channels)
    normed = rms_scaled(tok[...], ngain_ref[...]).astype(BF16)
    kv[me] = normed

    pl.semaphore_wait(barrier, rows * cols - 1)

    def push(slot, row, col, send_sem):
        return pltpu.make_async_remote_copy(
            src_ref=kv.at[slot], dst_ref=kv.at[slot], send_sem=send_sem, recv_sem=recv_sem.at[slot],
            device_id=(v, row, col), device_id_type=MESH,
        )

    def z_copy(k):
        return push(me, (r + rows - k) % rows, c, z_send.at[k])

    def x_copy(k, d):
        slot = ((r + k) % rows) * cols + c
        return push(slot, r, ((x + d) % nx) * 2 + lane, x_send.at[k, d])

    def d_copy(k, d):
        slot = ((r + k) % rows) * cols + ((x + d) % nx) * 2 + lane
        return push(slot, r, sibling, d_send.at[k, d])

    def arrived(slot):
        push(slot, r, sibling, d_send.at[0, 0]).wait_recv()

    def spread(k):
        for d in range(1, nx):
            x_copy(k, d).start()
        d_copy(k, 0).start()

    for k in range(1, rows):
        z_copy(k).start()
    spread(0)

    def halo_copies(phase, first, times):
        span = pl.ds(first, times)
        jobs = []
        for side, dr in ((0, 1), (1, -1)):
            jobs.append((row_out.at[span, side], row_in.at[span, side], dr, 0, side))
        for side, dc in ((0, 1), (1, -1)):
            edge = pl.ds(count - 16 if side == 0 else 0, 16)
            for dr in (-1, 0, 1):
                jobs.append((flat.at[span, edge], col_in.at[span, side, 1 - dr], dr, dc, 3 + side * 3 + dr))
        made = []
        for src, dst, dr, dc, n in jobs:
            to_row, to_col, from_row, from_col = r + dr, c + dc, r - dr, c - dc
            sends = (to_row >= 0) & (to_row < rows) & (to_col >= 0) & (to_col < cols)
            gets = (from_row >= 0) & (from_row < rows) & (from_col >= 0) & (from_col < cols)
            copy = pltpu.make_async_remote_copy(
                src_ref=src, dst_ref=dst, send_sem=halo_send.at[phase, n], recv_sem=halo_recv.at[phase, n],
                device_id=(v, lax.select(sends, to_row, r), lax.select(sends, to_col, c)), device_id_type=MESH,
            )
            made.append((copy, dst, sends, gets))
        return made

    def place(t, values):
        flat[t] = values.astype(BF16)
        blank = jnp.zeros((row_out.shape[2] - tile_cols, 128), F32)
        for n, lanes in parts:
            for q in range(tile_cols):
                pad[t, n, pl.ds((q + 1) * 16 + 8, 8), :] = values[q * 8 : q * 8 + 8, lanes]
            for side, at in ((0, 15), (1, 8)):
                line = pad[t, n, pl.ds(16 + at, tile_cols, stride=16), :]
                row_out[t, side, :, lanes] = jnp.concatenate([line, blank], axis=0).astype(BF16)

    def send_halo(copies):
        for copy, dst, sends, gets in copies:
            pl.when(sends)(copy.start)

            @pl.when(jnp.logical_not(gets))
            def _(dst=dst):
                dst[...] = jnp.zeros(dst.shape, BF16)

    def take_halo(copies):
        for copy, dst, sends, gets in copies:
            pl.when(gets)(copy.wait_recv)

    def end_halo(copies):
        for copy, dst, sends, gets in copies:
            pl.when(sends)(copy.wait_send)

    def insert_halo(t):
        for n, lanes in parts:
            for side, (col, base) in enumerate(((0, 8), (tile_cols + 1, 0))):
                above, beside, below = (col_in[t, side, near, :, lanes].astype(F32) for near in range(3))
                pad[t, n, pl.ds(col * 16 + 8, 8), :] = beside[base : base + 8]
                pad[t, n, pl.ds(col * 16 + 7, 1), :] = above[base + 7 : base + 8]
                pad[t, n, pl.ds(col * 16 + 16, 1), :] = below[base : base + 1]
            for side, at in ((0, 7), (1, 16)):
                pad[t, n, pl.ds(16 + at, tile_cols, stride=16), :] = row_in[t, side, :, lanes].astype(F32)[:tile_cols]
            for i in range(3):
                lines = [pad[t, n, pl.ds(q * 16 + 7 + i, 8), :] for q in range(tile_cols + 2)]
                for m in range(tile_cols // 2 + 1):
                    both = jnp.concatenate(lines[2 * m : 2 * m + 2], axis=0)
                    even[t, i, pl.ds(m * 16, 16), lanes] = both.astype(BF16)
                for m in range(tile_cols // 2):
                    both = jnp.concatenate(lines[2 * m + 1 : 2 * m + 3], axis=0)
                    odd[t, i, pl.ds(m * 16, 16), lanes] = both.astype(BF16)

    def convolve(t):
        result = None
        for i in range(3):
            for j in range(3):
                window = odd[t, i] if j == 1 else even[t, i, pl.ds(j * 8, count), :]
                part = jnp.dot(window, wc[t, i, j], preferred_element_type=F32)
                result = part if result is None else result + part
        return result

    loads[0].wait()
    for t in range(2):
        place(t, cache[t].astype(F32).reshape(count, channels))
    cache_halo = halo_copies(0, 0, 2)
    send_halo(cache_halo)

    loads[1].wait()
    loads[2].wait()
    query = (jnp.dot(normed, wq[...], preferred_element_type=F32) * (1.0 / math.sqrt(channels))).astype(BF16)
    qk[...] = lax.dot_general(query, wk[...], (((1,), (1,)), ((), ())), preferred_element_type=F32).astype(BF16)
    peak[...] = jnp.full(peak.shape, -1e30, F32)
    total[...] = jnp.zeros(total.shape, F32)
    acc[...] = jnp.zeros(acc.shape, F32)

    take_halo(cache_halo)
    loads[3].wait()
    insert_halo(0)
    insert_halo(1)
    sums[...] = convolve(0) + convolve(1)

    def cross(k):
        for d in range(1, nx):
            arrived(((r + k) % rows) * cols + ((x + d) % nx) * 2 + lane)
            d_copy(k, d).start()

    def attend(k):
        row = (r + k) % rows
        for d in range(nx):
            arrived(row * cols + d * 2 + 1 - lane)
        keys = kv[pl.ds(row * cols, cols)].reshape(cols * count, channels)
        scores = lax.dot_general(qk[...], keys, (((1,), (1,)), ((), ())), preferred_element_type=F32)
        old = peak[:, :1]
        new = jnp.maximum(old, jnp.max(scores, axis=1, keepdims=True))
        weights = jnp.exp(scores - new)
        scale = jnp.exp(old - new)
        total[...] = jnp.broadcast_to(total[:, :1] * scale + jnp.sum(weights, axis=1, keepdims=True), total.shape)
        acc[...] = acc[...] * scale + jnp.dot(weights.astype(BF16), keys, preferred_element_type=F32)
        peak[...] = jnp.broadcast_to(new, peak.shape)

    @pl.loop(1, rows)
    def _(k):
        arrived(((r + k) % rows) * cols + c)
        spread(k)
        cross(k - 1)
        attend(k - 1)

    cross(rows - 1)
    attend(rows - 1)

    loads[4].wait()
    loads[5].wait()
    pooled = (acc[...] / total[:, :1]).astype(BF16)
    attended = jnp.dot(pooled, wv[...], preferred_element_type=F32).astype(BF16)
    hidden = (tok[...] + jnp.dot(attended, wo[...], preferred_element_type=F32)).astype(BF16)
    hidden32 = hidden.astype(F32)
    scaled = rms_scaled(hidden32, cgain_ref[...])
    place(2, scaled / (1.0 + jnp.exp(-scaled)))
    frame_halo = halo_copies(1, 2, 1)
    send_halo(frame_halo)
    hidden_ref[...] = hidden32.reshape(hidden_ref.shape).astype(BF16)
    sums[...] += hidden32[:, :out_channels] + bias_ref[...]
    take_halo(frame_halo)
    insert_halo(2)
    mixed_ref[...] = (sums[...] + convolve(2)).reshape(mixed_ref.shape).astype(BF16)

    end_halo(cache_halo)
    end_halo(frame_halo)
    for k in range(1, rows):
        z_copy(k).wait_send()

    @pl.loop(0, rows)
    def _(k):
        for d in range(1, nx):
            x_copy(k, d).wait_send()
        for d in range(nx):
            d_copy(k, d).wait_send()


def solution(mesh):
    rows, cols = mesh.shape["rows"], mesh.shape["cols"]

    def body(frame_in, norm_gain, w_query, w_key, w_value, w_out, conv_gain, conv_cache, w_conv, conv_bias):
        tile_rows, tile_cols, channels = frame_in.shape
        out_channels = w_conv.shape[-1]
        count = tile_rows * tile_cols
        edge = -(-tile_cols // 16) * 16
        frame_in = frame_in.transpose(1, 0, 2)
        conv_cache = conv_cache.transpose(0, 2, 1, 3)
        vmem, held = pl.BlockSpec(memory_space=pltpu.VMEM), pl.BlockSpec(memory_space=pl.ANY)
        dma = pltpu.SemaphoreType.DMA
        square = pltpu.VMEM((channels, channels), BF16)
        hidden, mixed_out = pl.pallas_call(
            functools.partial(kernel, rows, cols),
            out_shape=(
                jax.ShapeDtypeStruct(frame_in.shape, BF16),
                jax.ShapeDtypeStruct((tile_cols, tile_rows, out_channels), BF16),
            ),
            in_specs=[vmem, vmem, held, held, held, held, vmem, held, held, vmem],
            out_specs=(vmem, vmem),
            scratch_shapes=[
                square, square, square, square,
                pltpu.VMEM(w_conv.shape, BF16),
                pltpu.VMEM(conv_cache.shape, BF16),
                pltpu.VMEM((rows * cols, count, channels), BF16),
                pltpu.VMEM((count, channels), F32),
                pltpu.VMEM((count, channels), BF16),
                pltpu.VMEM((count, channels), F32),
                pltpu.VMEM((count, 128), F32),
                pltpu.VMEM((count, 128), F32),
                pltpu.VMEM((3, channels // 128, (tile_cols + 3) * 16, 128), F32),
                pltpu.VMEM((3, count, channels), BF16),
                pltpu.VMEM((3, 2, edge, channels), BF16),
                pltpu.VMEM((3, 2, edge, channels), BF16),
                pltpu.VMEM((3, 2, 3, 16, channels), BF16),
                pltpu.VMEM((3, 3, count + 16, channels), BF16),
                pltpu.VMEM((3, 3, count, channels), BF16),
                pltpu.VMEM((count, out_channels), F32),
                dma((6,)), dma((rows,)), dma((rows, cols // 2)), dma((rows, cols // 2)), dma((rows * cols,)),
                dma((2, 8)), dma((2, 8)),
            ],
            compiler_params=pltpu.CompilerParams(
                collective_id=0, has_side_effects=True, vmem_limit_bytes=56 * 1024 * 1024
            ),
        )(
            frame_in, norm_gain.reshape(1, channels), w_query, w_key, w_value, w_out,
            conv_gain.reshape(1, channels), conv_cache, w_conv, conv_bias.reshape(1, out_channels),
        )
        return hidden.transpose(1, 0, 2), mixed_out.transpose(1, 0, 2)

    tiles = P(("video", "rows"), "cols", None)
    in_specs = (tiles, P(), P(), P(), P(), P(), P(), P(None, ("video", "rows"), "cols", None), P(), P())
    return jax.shard_map(body, mesh=mesh, in_specs=in_specs, out_specs=(tiles, tiles), check_vma=False)
```

```python
import functools
import math

import jax
import jax.numpy as jnp
from jax import lax
from jax.experimental import pallas as pl
from jax.experimental.pallas import tpu as pltpu
from jax.sharding import PartitionSpec as P

MESH = pl.DeviceIdType.MESH
F32 = jnp.float32
BF16 = jnp.bfloat16


def rms_scaled(values, gain):
    mean_sq = jnp.mean(values * values, axis=-1, keepdims=True)
    return values * lax.rsqrt(mean_sq + 1e-06) * gain


def kernel(
    rows, cols, frame_ref, ngain_ref, wq_hbm, wk_hbm, wv_hbm, wo_hbm, cgain_ref, cache_hbm, wc_hbm, bias_ref,
    hidden_ref, mixed_ref,
    wq, wk, wv, wo, wc, cache, kv, tok, qk, acc, peak, total, pad, flat, row_out, row_in, col_in, even, odd, sums,
    load_sem, z_send, x_send, d_send, recv_sem, halo_send, halo_recv,
):
    tile_cols, tile_rows, channels = frame_ref.shape
    out_channels = wc.shape[-1]
    count = tile_rows * tile_cols
    v, r, c = lax.axis_index("video"), lax.axis_index("rows"), lax.axis_index("cols")
    nx = cols // 2
    x, lane = c // 2, c % 2
    sibling = x * 2 + 1 - lane
    me = r * cols + c
    parts = [(n, slice(n * 128, n * 128 + 128)) for n in range(channels // 128)]

    loads = [
        pltpu.make_async_copy(src, dst, load_sem.at[n])
        for n, (src, dst) in enumerate(
            [(cache_hbm, cache), (wq_hbm, wq), (wk_hbm, wk), (wc_hbm, wc), (wv_hbm, wv), (wo_hbm, wo)]
        )
    ]
    for load in loads:
        load.start()

    barrier = pltpu.get_barrier_semaphore()

    near = [(r + dr, c + dc) for dr in (-1, 0, 1) for dc in (-1, 0, 1) if dr or dc]
    peers = [((row >= 0) & (row < rows) & (col >= 0) & (col < cols), row, col) for row, col in near]
    peers += [(None, r, ((x + d) % nx) * 2 + lane) for d in range(1, nx)]
    for there, row, col in peers:

        def greet(row=row, col=col):
            pl.semaphore_signal(barrier, inc=1, device_id=(v, row, col), device_id_type=MESH)

        greet() if there is None else pl.when(there)(greet)

    tok[...] = frame_ref[...].astype(F32).reshape(count, channels)
    normed = rms_scaled(tok[...], ngain_ref[...]).astype(BF16)
    kv[me] = normed

    tall = 1 + (r > 0).astype(jnp.int32) + (r + 1 < rows).astype(jnp.int32)
    broad = 1 + (c > 0).astype(jnp.int32) + (c + 1 < cols).astype(jnp.int32)
    pl.semaphore_wait(barrier, tall * broad - 1 + nx - 1)

    half = count // 2

    def push(slot, h, row, col, send_sem):
        piece = kv.at[slot, pl.ds(h * half, half)]
        return pltpu.make_async_remote_copy(
            src_ref=piece, dst_ref=piece, send_sem=send_sem, recv_sem=recv_sem.at[slot, h],
            device_id=(v, row, col), device_id_type=MESH,
        )

    def z_copy(row, h, way):
        return push(row * cols + c, h, r + (1 if way == 0 else -1), c, z_send.at[way, row, h])

    def x_copy(row, h, d):
        return push(row * cols + c, h, r, ((x + d) % nx) * 2 + lane, x_send.at[row, d, h])

    def d_copy(row, h, d):
        return push(row * cols + ((x + d) % nx) * 2 + lane, h, r, sibling, d_send.at[row, d, h])

    def arrived(slot, h):
        push(slot, h, r, sibling, d_send.at[0, 0, 0]).wait_recv()

    def can_pass(way):
        return r + 1 < rows if way == 0 else r > 0

    def spread(row, h, ways):
        for way in ways:
            pl.when(can_pass(way))(lambda way=way: z_copy(row, h, way).start())
        for d in range(1, nx):
            x_copy(row, h, d).start()
        d_copy(row, h, 0).start()

    def source(k, way):
        row = r - k if way == 0 else r + k
        return row, (row >= 0) & (row < rows)

    for h in range(2):
        spread(r, h, (0, 1))

    def halo_copies(phase, first, times):
        span = pl.ds(first, times)
        jobs = []
        for side, dr in ((0, 1), (1, -1)):
            jobs.append((row_out.at[span, side], row_in.at[span, side], dr, 0, side))
        for side, dc in ((0, 1), (1, -1)):
            edge = pl.ds(count - 16 if side == 0 else 0, 16)
            for dr in (-1, 0, 1):
                jobs.append((flat.at[span, edge], col_in.at[span, side, 1 - dr], dr, dc, 3 + side * 3 + dr))
        made = []
        for src, dst, dr, dc, n in jobs:
            to_row, to_col, from_row, from_col = r + dr, c + dc, r - dr, c - dc
            sends = (to_row >= 0) & (to_row < rows) & (to_col >= 0) & (to_col < cols)
            gets = (from_row >= 0) & (from_row < rows) & (from_col >= 0) & (from_col < cols)
            copy = pltpu.make_async_remote_copy(
                src_ref=src, dst_ref=dst, send_sem=halo_send.at[phase, n], recv_sem=halo_recv.at[phase, n],
                device_id=(v, lax.select(sends, to_row, r), lax.select(sends, to_col, c)), device_id_type=MESH,
            )
            made.append((copy, dst, sends, gets))
        return made

    def place(t, values):
        flat[t] = values.astype(BF16)
        blank = jnp.zeros((row_out.shape[2] - tile_cols, 128), F32)
        for n, lanes in parts:
            for q in range(tile_cols):
                pad[t, n, pl.ds((q + 1) * 16 + 8, 8), :] = values[q * 8 : q * 8 + 8, lanes]
            for side, at in ((0, 15), (1, 8)):
                line = pad[t, n, pl.ds(16 + at, tile_cols, stride=16), :]
                row_out[t, side, :, lanes] = jnp.concatenate([line, blank], axis=0).astype(BF16)

    def send_halo(copies):
        for copy, dst, sends, gets in copies:
            pl.when(sends)(copy.start)

            @pl.when(jnp.logical_not(gets))
            def _(dst=dst):
                dst[...] = jnp.zeros(dst.shape, BF16)

    def take_halo(copies):
        for copy, dst, sends, gets in copies:
            pl.when(gets)(copy.wait_recv)

    def end_halo(copies):
        for copy, dst, sends, gets in copies:
            pl.when(sends)(copy.wait_send)

    def insert_halo(t):
        for n, lanes in parts:
            for side, (col, base) in enumerate(((0, 8), (tile_cols + 1, 0))):
                above, beside, below = (col_in[t, side, near, :, lanes].astype(F32) for near in range(3))
                pad[t, n, pl.ds(col * 16 + 8, 8), :] = beside[base : base + 8]
                pad[t, n, pl.ds(col * 16 + 7, 1), :] = above[base + 7 : base + 8]
                pad[t, n, pl.ds(col * 16 + 16, 1), :] = below[base : base + 1]
            for side, at in ((0, 7), (1, 16)):
                pad[t, n, pl.ds(16 + at, tile_cols, stride=16), :] = row_in[t, side, :, lanes].astype(F32)[:tile_cols]
            for i in range(3):
                lines = [pad[t, n, pl.ds(q * 16 + 7 + i, 8), :] for q in range(tile_cols + 2)]
                for m in range(tile_cols // 2 + 1):
                    both = jnp.concatenate(lines[2 * m : 2 * m + 2], axis=0)
                    even[t, i, pl.ds(m * 16, 16), lanes] = both.astype(BF16)
                for m in range(tile_cols // 2):
                    both = jnp.concatenate(lines[2 * m + 1 : 2 * m + 3], axis=0)
                    odd[t, i, pl.ds(m * 16, 16), lanes] = both.astype(BF16)

    def convolve(t):
        result = None
        for i in range(3):
            for j in range(3):
                window = odd[t, i] if j == 1 else even[t, i, pl.ds(j * 8, count), :]
                part = jnp.dot(window, wc[t, i, j], preferred_element_type=F32)
                result = part if result is None else result + part
        return result

    loads[0].wait()
    for t in range(2):
        place(t, cache[t].astype(F32).reshape(count, channels))
    cache_halo = halo_copies(0, 0, 2)
    send_halo(cache_halo)

    loads[1].wait()
    loads[2].wait()
    query = (jnp.dot(normed, wq[...], preferred_element_type=F32) * (1.0 / math.sqrt(channels))).astype(BF16)
    qk[...] = lax.dot_general(query, wk[...], (((1,), (1,)), ((), ())), preferred_element_type=F32).astype(BF16)
    peak[...] = jnp.full(peak.shape, -1e30, F32)
    total[...] = jnp.zeros(total.shape, F32)
    acc[...] = jnp.zeros(acc.shape, F32)

    def pass_on(k):
        for way in range(2):
            row, valid = source(k, way)

            @pl.when(valid)
            def _(row=row, way=way):
                for h in range(2):
                    arrived(row * cols + c, h)
                    spread(row, h, (way,))

    def cross(row):
        for d in range(1, nx):
            for h in range(2):
                arrived(row * cols + ((x + d) % nx) * 2 + lane, h)
                d_copy(row, h, d).start()

    def attend(row):
        for d in range(nx):
            for h in range(2):
                arrived(row * cols + d * 2 + 1 - lane, h)
        keys = kv[pl.ds(row * cols, cols)].reshape(cols * count, channels)
        scores = lax.dot_general(qk[...], keys, (((1,), (1,)), ((), ())), preferred_element_type=F32)
        old = peak[:, :1]
        new = jnp.maximum(old, jnp.max(scores, axis=1, keepdims=True))
        weights = jnp.exp(scores - new)
        scale = jnp.exp(old - new)
        total[...] = jnp.broadcast_to(total[:, :1] * scale + jnp.sum(weights, axis=1, keepdims=True), total.shape)
        acc[...] = acc[...] * scale + jnp.dot(weights.astype(BF16), keys, preferred_element_type=F32)
        peak[...] = jnp.broadcast_to(new, peak.shape)

    def finish(k):
        for way in range(2):
            row, valid = source(k, way)

            @pl.when(valid)
            def _(row=row):
                cross(row)
                attend(row)

    pass_on(1)
    take_halo(cache_halo)
    loads[3].wait()
    insert_halo(0)
    insert_halo(1)
    sums[...] = convolve(0)
    cross(r)
    attend(r)

    @pl.loop(2, rows)
    def _(k):
        pass_on(k)

        @pl.when(k == 2)
        def _():
            sums[...] += convolve(1)

        finish(k - 1)

    if rows <= 2:
        sums[...] += convolve(1)
    finish(rows - 1)

    loads[4].wait()
    loads[5].wait()
    pooled = (acc[...] / total[:, :1]).astype(BF16)
    attended = jnp.dot(pooled, wv[...], preferred_element_type=F32).astype(BF16)
    hidden = (tok[...] + jnp.dot(attended, wo[...], preferred_element_type=F32)).astype(BF16)
    hidden32 = hidden.astype(F32)
    scaled = rms_scaled(hidden32, cgain_ref[...])
    place(2, scaled / (1.0 + jnp.exp(-scaled)))
    frame_halo = halo_copies(1, 2, 1)
    send_halo(frame_halo)
    hidden_ref[...] = hidden32.reshape(hidden_ref.shape).astype(BF16)
    sums[...] += hidden32[:, :out_channels] + bias_ref[...]
    take_halo(frame_halo)
    insert_halo(2)
    mixed_ref[...] = (sums[...] + convolve(2)).reshape(mixed_ref.shape).astype(BF16)

    end_halo(cache_halo)
    end_halo(frame_halo)
    @pl.loop(0, rows)
    def _(row):
        for h in range(2):
            for way in range(2):

                @pl.when(can_pass(way) & (row <= r if way == 0 else row >= r))
                def _(h=h, way=way):
                    z_copy(row, h, way).wait_send()

            for d in range(1, nx):
                x_copy(row, h, d).wait_send()
            for d in range(nx):
                d_copy(row, h, d).wait_send()


def solution(mesh):
    rows, cols = mesh.shape["rows"], mesh.shape["cols"]

    def body(frame_in, norm_gain, w_query, w_key, w_value, w_out, conv_gain, conv_cache, w_conv, conv_bias):
        tile_rows, tile_cols, channels = frame_in.shape
        out_channels = w_conv.shape[-1]
        count = tile_rows * tile_cols
        edge = -(-tile_cols // 16) * 16
        frame_in = frame_in.transpose(1, 0, 2)
        conv_cache = conv_cache.transpose(0, 2, 1, 3)
        vmem, held = pl.BlockSpec(memory_space=pltpu.VMEM), pl.BlockSpec(memory_space=pl.ANY)
        dma = pltpu.SemaphoreType.DMA
        square = pltpu.VMEM((channels, channels), BF16)
        hidden, mixed_out = pl.pallas_call(
            functools.partial(kernel, rows, cols),
            out_shape=(
                jax.ShapeDtypeStruct(frame_in.shape, BF16),
                jax.ShapeDtypeStruct((tile_cols, tile_rows, out_channels), BF16),
            ),
            in_specs=[vmem, vmem, held, held, held, held, vmem, held, held, vmem],
            out_specs=(vmem, vmem),
            scratch_shapes=[
                square, square, square, square,
                pltpu.VMEM(w_conv.shape, BF16),
                pltpu.VMEM(conv_cache.shape, BF16),
                pltpu.VMEM((rows * cols, count, channels), BF16),
                pltpu.VMEM((count, channels), F32),
                pltpu.VMEM((count, channels), BF16),
                pltpu.VMEM((count, channels), F32),
                pltpu.VMEM((count, 128), F32),
                pltpu.VMEM((count, 128), F32),
                pltpu.VMEM((3, channels // 128, (tile_cols + 3) * 16, 128), F32),
                pltpu.VMEM((3, count, channels), BF16),
                pltpu.VMEM((3, 2, edge, channels), BF16),
                pltpu.VMEM((3, 2, edge, channels), BF16),
                pltpu.VMEM((3, 2, 3, 16, channels), BF16),
                pltpu.VMEM((3, 3, count + 16, channels), BF16),
                pltpu.VMEM((3, 3, count, channels), BF16),
                pltpu.VMEM((count, out_channels), F32),
                dma((6,)), dma((2, rows, 2)), dma((rows, cols // 2, 2)), dma((rows, cols // 2, 2)), dma((rows * cols, 2)),
                dma((2, 8)), dma((2, 8)),
            ],
            compiler_params=pltpu.CompilerParams(
                collective_id=0, has_side_effects=True, vmem_limit_bytes=56 * 1024 * 1024
            ),
        )(
            frame_in, norm_gain.reshape(1, channels), w_query, w_key, w_value, w_out,
            conv_gain.reshape(1, channels), conv_cache, w_conv, conv_bias.reshape(1, out_channels),
        )
        return hidden.transpose(1, 0, 2), mixed_out.transpose(1, 0, 2)

    tiles = P(("video", "rows"), "cols", None)
    in_specs = (tiles, P(), P(), P(), P(), P(), P(), P(None, ("video", "rows"), "cols", None), P(), P())
    return jax.shard_map(body, mesh=mesh, in_specs=in_specs, out_specs=(tiles, tiles), check_vma=False)
```
